32 devices in a mesh: dp: 32 (over z, y, x, core).
Axes of the slice: x: 2, y: 2, z: 4, core: 2. Of those that a mesh axis runs over, the one named last changes fastest.
Arguments:
- tokens: float32 [8192, 1024], P('dp'), may hold values from -6 to 6
- cotangent: float32 [8192, 1024], P('dp'), may hold values from -6 to 6
- weight: float32 [1024, 1024], replicated, may hold values from -0.1875 to 0.1875
- first_moment: float32 [1024, 1024], P('dp'), may hold values from -0.6 to 0.6
- second_moment: float32 [1024, 1024], P('dp'), may hold values from 0.001 to 0.1
Outputs:
- projected: float32 [8192, 1024], P('dp')
- input_grad: float32 [8192, 1024], P('dp')
- new_weight: float32 [1024, 1024], replicated
- new_first: float32 [1024, 1024], P('dp')
- new_second: float32 [1024, 1024], P('dp')
- next_projected: float32 [8192, 1024], P('dp')
The draws below stay inside these ranges and needn't reach their ends.
All inputs are finite; a program needn't handle non-finite values.
Results may differ from the reference program's by a relative error of at most 0.00017.
Values sent between devices are 32-bit elements; how exact they have to be, the bound alone decides.
No kernel may reach another device: no remote copies, remote signals or barrier semaphores. Data moves between devices by JAX's collectives and lax.ppermute only.
A program may use at most 64 MiB of HBM per device.

```python
import math
import jax
import jax.numpy as jnp
from jax import lax

D = 1024
TOK_DEV = 256
TOKENS = 8192
N_DP = 32


def raised(result, own_key, source, target, blocks, factor):
    def block_of(dim):
        return (jnp.arange(result.shape[dim]) // (result.shape[dim] // blocks)).reshape((-1,) + (1,) * (result.ndim - 1 - dim))

    one_side = jax.random.permutation(own_key, blocks)[block_of(target)]
    far = (block_of(target) + blocks // 2) % blocks
    return jnp.where((block_of(source) == one_side) | (block_of(source) == far), factor * result, result)


def block_scale(key, dims, split, smallest, high):
    gain, own = 1.0, jax.random.fold_in(key, 6)
    for axis_at, parts in split:
        draws = jnp.exp(jax.random.uniform(jax.random.fold_in(own, axis_at), (parts,), jnp.float32, smallest / len(split), high / len(split)))
        gain = gain * jnp.repeat(draws, dims[axis_at] // parts).reshape([-1 if axis == axis_at else 1 for axis in range(len(dims))])
    return gain


def bell_draw(rng, shape, spread, reach, split=(), held_as=jnp.bfloat16):
    values = jax.random.normal(rng, shape, jnp.float32) * spread
    if len(split) > 0:
        values = block_scale(rng, shape, split, -0.22, 0.18) * values
    return jnp.clip(values, min=-reach, max=reach).astype(held_as)


def noise_with(own_key, extent, deviation, limit, shards, heavy, held_as=jnp.bfloat16):
    values = deviation * jax.random.normal(own_key, extent, jnp.float32)
    if shards:
        values = values * block_scale(own_key, extent, shards, -0.22, 0.18)
    return jnp.clip(raised(values, jax.random.fold_in(own_key, 3), *heavy), -limit, limit).astype(held_as)


def setup_inputs(seed: int = 0) -> dict:
    streams_of = jax.random.split(jax.random.key(seed), 6)
    tokens = noise_with(streams_of[0], (TOKENS, D), 1.0, 6.0, ((0, 32),), (0, 1, 32, 2.75), jnp.float32)
    cotangent = bell_draw(streams_of[1], (TOKENS, D), 1.0, 6.0, ((0, 32),), jnp.float32)
    weight = bell_draw(streams_of[2], (D, D), D ** -0.5, 0.1875, (), jnp.float32)
    first_moment = bell_draw(streams_of[3], (D, D), 0.1, 0.6, ((0, 32),), jnp.float32)
    second_moment = jnp.clip(jnp.exp(math.log(0.1) - 4.6051702 * jax.random.uniform(streams_of[4], (D, D), jnp.float32) ** block_scale(streams_of[4], (D, D), ((0, 32),), -0.2, 0.2)), 0.001, 0.1)
    return dict(tokens=tokens, cotangent=cotangent, weight=weight, first_moment=first_moment, second_moment=second_moment)


beta_one = 0.9
beta_two = 0.999
rate_value = 0.01
step_count = 10
adam_epsilon = 1e-08
norm_epsilon = 1e-06

def combine(left_rows, right_rows):
    cross_term = lax.optimization_barrier(jnp.sum(left_rows * right_rows, axis=-1, keepdims=True))
    left_norm = lax.optimization_barrier(jnp.sum(left_rows * left_rows, axis=-1, keepdims=True))
    right_norm = lax.optimization_barrier(jnp.sum(right_rows * right_rows, axis=-1, keepdims=True))
    left_coef = 1.0 - cross_term / (2.0 * (left_norm + norm_epsilon))
    right_coef = 1.0 - cross_term / (2.0 * (right_norm + norm_epsilon))
    return left_coef * left_rows + right_coef * right_rows

def adam_update(gradient, weight_rows, first_rows, second_rows):
    first_new = beta_one * first_rows + (1.0 - beta_one) * gradient
    second_new = beta_two * second_rows + (1.0 - beta_two) * gradient * gradient
    first_hat = first_new / (1.0 - beta_one ** step_count)
    second_hat = second_new / (1.0 - beta_two ** step_count)
    weight_new = weight_rows - rate_value * first_hat / (jnp.sqrt(second_hat) + adam_epsilon)
    return (weight_new, first_new, second_new)

def reference(tokens, cotangent, weight, first_moment, second_moment):
    highest = lax.Precision.HIGHEST
    projected = jnp.dot(tokens, weight, precision=highest, preferred_element_type=jnp.float32)
    input_grad = lax.dot_general(cotangent, weight, (((1,), (1,)), ((), ())), precision=highest, preferred_element_type=jnp.float32)
    token_groups = tokens.reshape(N_DP, TOK_DEV, D)
    cotangent_groups = cotangent.reshape(N_DP, TOK_DEV, D)
    stride = 64 if D % 64 == 0 else D
    block_count = D // stride

    def block_rows(start):
        columns = lax.dynamic_slice_in_dim(token_groups, start, stride, 2)
        stacked = jnp.einsum('ntr,ntc->nrc', columns, cotangent_groups, precision=highest) / TOK_DEV
        while stacked.shape[0] > 1:
            halfway = stacked.shape[0] // 2
            stacked = combine(stacked[:halfway], stacked[halfway:])
        return stacked[0]
    starts = (jnp.arange(block_count) * stride).astype(jnp.int32)
    summed_grad = lax.map(block_rows, starts).reshape(D, D)
    new_weight, new_first, new_second = adam_update(summed_grad, weight, first_moment, second_moment)
    next_projected = jnp.dot(tokens, new_weight, precision=highest, preferred_element_type=jnp.float32)
    return (projected, input_grad, new_weight, new_first, new_second, next_projected)
```

```python
import functools
import jax
import jax.numpy as jnp
from jax import lax
from jax.experimental import pallas as pl
from jax.experimental.pallas import tpu as pltpu
from jax.sharding import PartitionSpec as P

beta_one = 0.9
beta_two = 0.999
rate_value = 0.01
step_count = 10
adam_epsilon = 1e-08
norm_epsilon = 1e-06

SIZES = (1,1,1,1)
FIRST_STREAM = 2

OWNER, TOP, MIDDLE, CORE, BITS = range(5)


def kernel_call(kernel, name, outs, megabytes, place, *arrays):
    vmem = pl.BlockSpec(memory_space=pltpu.VMEM)
    return pl.pallas_call(
        kernel,
        out_shape=tuple(outs),
        in_specs=[pl.BlockSpec(memory_space=pltpu.SMEM)] + [vmem] * len(arrays),
        out_specs=tuple(vmem for _ in outs),
        compiler_params=pltpu.CompilerParams(vmem_limit_bytes=megabytes << 20),
        cost_estimate=pl.CostEstimate(flops=1, bytes_accessed=1, transcendentals=0),
        name=name,
    )(place, *arrays)


def f32(*shape):
    return jax.ShapeDtypeStruct(shape, jnp.float32)


def bf16(*shape):
    return jax.ShapeDtypeStruct(shape, jnp.bfloat16)


def swapped(block, mask):
    count = lax.axis_size("dp")
    return lax.ppermute(block, "dp", [(i, i ^ mask) for i in range(count)])


def parts(x):
    high = x.astype(jnp.bfloat16)
    return high, (x - high.astype(jnp.float32)).astype(jnp.bfloat16)


def product(left, right, contract=0):
    left_high, left_low = left
    right_high, right_low = right

    def dot(a, b):
        return lax.dot_general(
            a, b, (((1,), (contract,)), ((), ())), preferred_element_type=jnp.float32
        )

    return dot(left_high, right_high) + (dot(left_high, right_low) + dot(left_low, right_high))


def combine(left_rows, right_rows):
    cross_term = jnp.sum(left_rows * right_rows, axis=-1, keepdims=True)
    left_norm = jnp.sum(left_rows * left_rows, axis=-1, keepdims=True)
    right_norm = jnp.sum(right_rows * right_rows, axis=-1, keepdims=True)
    left_coef = 1.0 - cross_term / (2.0 * (left_norm + norm_epsilon))
    right_coef = 1.0 - cross_term / (2.0 * (right_norm + norm_epsilon))
    return left_coef * left_rows + right_coef * right_rows


def adam_update(gradient, weight_rows, first_rows, second_rows):
    first_new = beta_one * first_rows + (1.0 - beta_one) * gradient
    second_new = beta_two * second_rows + (1.0 - beta_two) * gradient * gradient
    first_hat = first_new / (1.0 - beta_one**step_count)
    second_hat = second_new / (1.0 - beta_two**step_count)
    weight_new = weight_rows - rate_value * first_hat / (jnp.sqrt(second_hat) + adam_epsilon)
    return (weight_new, first_new, second_new)


def prepare_kernel(middle, own, spans, place_ref, tokens_ref, keep_ref, other_ref):
    def fill(mine):
        width = 128
        for base in range(0, tokens_ref.shape[1], width):
            block = tokens_ref[:, base : base + width].T
            for group in range(base // own, (base + width) // own):
                node, here = divmod(group, 2)
                top, mid = divmod(node, middle)
                target = keep_ref if here == mine else other_ref
                for first, piece in spans:
                    row = first * middle * 2 + (mid * 2 + top) * piece
                    low = group * own + first - base
                    target[row : row + piece, :] = block[low : low + piece, :]

    for mine in range(2):
        pl.when(place_ref[CORE] == mine)(functools.partial(fill, mine))


def choose_kernel(place_ref, cotangent_ref, swap_ref, send_ref):
    half = send_ref.shape[0]
    send_ref[...] = jnp.where(place_ref[OWNER] == 1, swap_ref[half:, :], cotangent_ref[:half, :])


def share_kernel(spans, place_ref, keep_ref, swap_ref, near_ref, *send_refs):
    owner = place_ref[OWNER] == 1
    near_ref[...] = jnp.where(owner, keep_ref[...], swap_ref[...])
    row = 0
    for send_ref in send_refs:
        rows = slice(row, row + send_ref.shape[0])
        send_ref[...] = jnp.where(owner, swap_ref[rows, :], keep_ref[rows, :])
        row += send_ref.shape[0]


def project_kernel(place_ref, tokens_ref, cotangent_ref, weight_ref, projected_ref, grad_ref):
    tokens = parts(tokens_ref[...])
    cotangent = parts(cotangent_ref[...])
    width = weight_ref.shape[0]
    step = min(256, width)
    for base in range(0, width, step):
        span = slice(base, base + step)
        projected_ref[:, span] = product(tokens, parts(weight_ref[:, span]))
        grad_ref[:, span] = product(cotangent, parts(weight_ref[span, :]), 1)


def near_kernel(scale, place_ref, tokens_ref, cotangent_ref, swap_ref, *near_refs):
    right = parts(jnp.where(place_ref[OWNER] == 1, cotangent_ref[...], swap_ref[...]))
    row = 0
    for near_ref in near_refs:
        rows = near_ref.shape[0]
        near_ref[...] = product(parts(tokens_ref[row : row + rows, :]), right) * scale
        row += rows


def assemble_kernel(place_ref, mine_ref, other_ref, high_ref, low_ref):
    owner = place_ref[OWNER] == 1
    half = mine_ref.shape[0]
    for at in range(2):
        chosen = jnp.where(owner == (at == 0), mine_ref[...], other_ref[...])
        rows = slice(at * half, (at + 1) * half)
        high_ref[rows, :], low_ref[rows, :] = parts(chosen)


def halves(place_ref, bit, half):
    mine = place_ref[BITS + bit]
    return [pl.ds(pl.multiple_of(part * half, half), half) for part in (mine, 1 - mine)]


def first_kernel(scale, bit, place_ref, near_ref, far_ref, high_ref, low_ref, keep_ref, send_ref):
    right = (high_ref[...], low_ref[...])
    for target, rows in zip((send_ref, keep_ref), halves(place_ref, bit, keep_ref.shape[0])[::-1]):
        target[...] = combine(near_ref[rows, :], product(parts(far_ref[rows, :]), right) * scale)


def middle_kernel(bit, place_ref, kept_ref, received_ref, keep_ref, send_ref):
    for target, rows in zip((send_ref, keep_ref), halves(place_ref, bit, keep_ref.shape[0])[::-1]):
        target[...] = combine(kept_ref[rows, :], received_ref[rows, :])


def merge_kernel(place_ref, kept_ref, received_ref, out_ref):
    out_ref[...] = combine(kept_ref[...], received_ref[...])


def last_kernel(
    first, place_ref, kept_ref, received_ref, weight_ref,
    own_first_ref, other_first_ref, own_second_ref, other_second_ref,
    weight_out, first_out, second_out,
):
    piece = first_out.shape[0]
    span = slice(first, first + piece)
    for top in range(2):
        mine = place_ref[TOP] == top
        rows = slice(top * piece, (top + 1) * piece)
        gradient = combine(kept_ref[rows, :], received_ref[rows, :])
        weight_new, first_new, second_new = adam_update(
            gradient,
            weight_ref[top, span, :],
            jnp.where(mine, own_first_ref[span, :], other_first_ref[span, :]),
            jnp.where(mine, own_second_ref[span, :], other_second_ref[span, :]),
        )
        weight_out[rows, :] = weight_new

        @pl.when(mine)
        def _():
            first_out[...] = first_new
            second_out[...] = second_new


def finish_kernel(middle, own, streams, place_ref, tokens_ref, *refs):
    *block_refs, weight_ref, projected_ref = refs
    mid, core = place_ref[MIDDLE], place_ref[CORE]
    for at, block_ref in enumerate(block_refs):
        stream, at = divmod(at, 2 * middle)
        far_mid, far_core = divmod(at, 2)
        device = (mid ^ far_mid) * 2 + (core ^ far_core)
        start = 0
        for first, piece in streams[stream]:
            for top in range(2):
                row = (device + top * middle * 2) * own + first
                weight_ref[pl.ds(pl.multiple_of(row, piece), piece), :] = block_ref[start : start + piece, :]
                start += piece
    depth = min(256, tokens_ref.shape[1])
    total = jnp.zeros(projected_ref.shape, jnp.float32)
    for base in range(0, tokens_ref.shape[1], depth):
        span = slice(base, base + depth)
        total = total + product(parts(tokens_ref[:, span]), parts(weight_ref[span, :]))
    projected_ref[...] = total


def tied(after, values):
    return list(lax.optimization_barrier((after, *values))[1:])


def chunk_order(sizes, levels):
    own = sum(sizes)
    fixed, ready, steps = 0.08 * own, {}, []
    free = [0.0] * levels
    for k, size in enumerate(sizes):
        ready[k, 0] = sum(sizes[: k + 1])
    for level in range(1, levels):
        cost = 1.0 if level == 1 else 0.5 if level == levels - 1 else 2.0 ** (1 - level)
        for k, size in enumerate(sizes):
            free[level] = max(free[level], ready[k, level - 1] + fixed) + cost * size
            ready[k, level] = free[level]
    return sorted(ready, key=lambda step: (ready[step], step[1]))


def relative_blocks(rows, order):
    blocks = {0: rows}
    for bit in order:
        for mask in list(blocks):
            blocks[mask | 1 << bit] = swapped(blocks[mask], 1 << bit)
    return blocks


def on_device(tokens, cotangent, weight, first_moment, second_moment):
    token_count, width = tokens.shape
    devices = lax.axis_size("dp")
    levels = devices.bit_length() - 1
    index = lax.axis_index("dp")
    own = width // devices
    middle = devices // 4
    quarter = own // 4
    sizes = [quarter * part for part in SIZES] if own % 32 == 0 else [own]
    spans = [(sum(sizes[:k]), sizes[k]) for k in range(len(sizes))]
    streams = [spans[:FIRST_STREAM], spans[FIRST_STREAM:]] if len(spans) > 1 else [spans]
    top_mask = devices >> 1
    core, top = index & 1, index >> levels - 1
    scale = 1.0 / token_count
    place = jnp.stack(
        [(core == top).astype(jnp.int32), top, index >> 1 & middle - 1, core]
        + [index >> bit & 1 for bit in range(levels)]
    )
    half_rows = width // 2

    cotangent_swap = swapped(cotangent, 1)
    tokens_keep, tokens_other = kernel_call(
        functools.partial(prepare_kernel, middle, own, spans), "prepare",
        [f32(half_rows, token_count)] * 2, 4, place, tokens,
    )
    tokens_swap = swapped(tokens_other, 1)
    (send_cotangent,) = kernel_call(
        choose_kernel, "choose", [f32(token_count // 2, width)], 4, place, cotangent, cotangent_swap
    )
    far_mine = swapped(send_cotangent, top_mask)
    near_tokens, *send_tokens = kernel_call(
        functools.partial(share_kernel, spans), "share",
        [f32(half_rows, token_count)] + [f32(2 * middle * piece, token_count) for _, piece in spans],
        4, place, tokens_keep, tokens_swap,
    )
    far_tokens = [swapped(block, top_mask) for block in send_tokens]
    other_first = swapped(first_moment, top_mask)
    other_second = swapped(second_moment, top_mask)

    near = kernel_call(
        functools.partial(near_kernel, scale), "near",
        [f32(2 * middle * piece, width) for _, piece in spans], 12, place, near_tokens, cotangent, cotangent_swap,
    )
    projected, input_grad = kernel_call(
        project_kernel, "project", [f32(token_count, width)] * 2, 20, place, tokens, cotangent, weight
    )
    weight_rows = lax.dynamic_index_in_dim(
        weight.reshape(2, devices // 2, own, width), index % (devices // 2), 1, keepdims=False
    )
    near, projected, input_grad, weight_rows, far_mine, far_tokens[0] = lax.optimization_barrier(
        (near, projected, input_grad, weight_rows, far_mine, far_tokens[0])
    )
    far_high, far_low = kernel_call(
        assemble_kernel, "assemble", [bf16(token_count, width)] * 2, 6, place, far_mine, swapped(far_mine, 1)
    )

    bits = list(range(levels - 2, 0, -1)) + [levels - 1]
    state, outs, after = {}, {}, far_high
    order = [(k, 0) for k in range(len(spans))] + [step for step in chunk_order(sizes, levels) if step[1] > 0]
    for at, (k, level) in enumerate(order):
        if at == len(spans):
            kept = [state[j][0] for j in range(len(spans))]
            after = lax.optimization_barrier(tuple(kept))[-1]
        if at == len(spans) + 2:
            after, other_first, other_second = lax.optimization_barrier((after, other_first, other_second))
        first, piece = spans[k]
        rows = 2 * piece * middle >> level + 1
        if level == 0:
            kernel, name, count = functools.partial(first_kernel, scale, bits[0]), "first", 2
            operands = [near[k], far_tokens[k], far_high, far_low]
        else:
            keep, send = state[k]
            operands = [keep, swapped(send, 1 << bits[level - 1])]
            if level < levels - 2:
                kernel, name, count = functools.partial(middle_kernel, bits[level]), "middle", 2
            elif level == levels - 2:
                kernel, name, count, rows = merge_kernel, "merge", 1, 2 * piece
        operands = tied(after, operands)
        if level < levels - 1:
            state[k] = kernel_call(kernel, name, [f32(rows, width)] * count, 8, place, *operands)
            state[k] = (state[k][0], state[k][-1])
            if level > 0:
                after = state[k][0]
        else:
            outs[k] = kernel_call(
                functools.partial(last_kernel, first), "last",
                [f32(2 * piece, width), f32(piece, width), f32(piece, width)], 4,
                place, *operands, weight_rows, first_moment, other_first, second_moment, other_second,
            )
            after = outs[k][0]
    outs = [outs[k] for k in range(len(spans))]
    new_rows, new_first, new_second = zip(*outs)
    new_first = jnp.concatenate(new_first, axis=0)
    new_second = jnp.concatenate(new_second, axis=0)

    if devices > 64:
        mine = jnp.concatenate(
            [lax.dynamic_slice_in_dim(x, top * (x.shape[0] // 2), x.shape[0] // 2, 0) for x in new_rows], axis=0
        )
        new_weight = lax.all_gather(mine, "dp", axis=0, tiled=True)
        next_projected = jnp.dot(
            tokens, new_weight, precision=lax.Precision.HIGH, preferred_element_type=jnp.float32
        )
        return (projected, input_grad, new_weight, new_first, new_second, next_projected)

    order = list(range(levels - 2, 0, -1))
    blocks = []
    for at, stream in enumerate(streams):
        rows = jnp.concatenate([new_rows[spans.index(span)] for span in stream], axis=0)
        found = relative_blocks(rows, order if at == 0 else order[::-1])
        for mid in range(middle):
            blocks += [found[mid << 1], swapped(found[mid << 1], 1)]
    new_weight, next_projected = kernel_call(
        functools.partial(finish_kernel, middle, own, streams), "finish",
        [f32(width, width), f32(token_count, width)], 28, place, tokens, *blocks,
    )
    return (projected, input_grad, new_weight, new_first, new_second, next_projected)


def solution(mesh):
    split, whole = P("dp", None), P()
    return jax.shard_map(
        on_device,
        mesh=mesh,
        in_specs=(split, split, whole, split, split),
        out_specs=(split, split, whole, split, split, split),
        check_vma=False,
    )
```

```python
import functools
import jax
import jax.numpy as jnp
from jax import lax
from jax.experimental import pallas as pl
from jax.experimental.pallas import tpu as pltpu
from jax.sharding import PartitionSpec as P

beta_one = 0.9
beta_two = 0.999
rate_value = 0.01
step_count = 10
adam_epsilon = 1e-08
norm_epsilon = 1e-06

MESSAGES = [[0], [1, 2, 3]]
GROUPS = [[0, 1], [2, 3]]
ORDER = [(0, 1), (1, 1), (0, 2), (1, 2), (0, 3), (1, 3), (0, 4), (1, 4)]
AHEAD = 1
JOIN, FRESH, DIRECT = True,False,0


OWNER, TOP, MIDDLE, CORE, BITS = range(5)


def kernel_call(kernel, name, outs, megabytes, place, *arrays, after=()):
    vmem = pl.BlockSpec(memory_space=pltpu.VMEM)
    count = 1 + len(arrays)

    def body(*refs):
        kernel(*refs[:count], *refs[count + len(after) :])

    return pl.pallas_call(
        body,
        out_shape=tuple(outs),
        in_specs=[pl.BlockSpec(memory_space=pltpu.SMEM)]
        + [vmem] * len(arrays)
        + [pl.BlockSpec(memory_space=pl.ANY)] * len(after),
        out_specs=tuple(vmem for _ in outs),
        compiler_params=pltpu.CompilerParams(vmem_limit_bytes=megabytes << 20),
        cost_estimate=pl.CostEstimate(flops=1, bytes_accessed=1, transcendentals=0),
        name=name,
    )(place, *arrays, *after)


def f32(*shape):
    return jax.ShapeDtypeStruct(shape, jnp.float32)


def bf16(*shape):
    return jax.ShapeDtypeStruct(shape, jnp.bfloat16)


def swapped(block, mask, owners=None):
    count = lax.axis_size("dp")
    high = count.bit_length() - 2
    return lax.ppermute(
        block, "dp", [(i, i ^ mask) for i in range(count) if owners is None or ((i & 1) == i >> high) == owners]
    )


def parts(x):
    high = x.astype(jnp.bfloat16)
    return high, (x - high.astype(jnp.float32)).astype(jnp.bfloat16)


def product(left, right, contract=0):
    left_high, left_low = left
    right_high, right_low = right

    def dot(a, b):
        return lax.dot_general(
            a, b, (((1,), (contract,)), ((), ())), preferred_element_type=jnp.float32
        )

    return dot(left_high, right_high) + (dot(left_high, right_low) + dot(left_low, right_high))


def combine(left_rows, right_rows):
    cross_term = jnp.sum(left_rows * right_rows, axis=-1, keepdims=True)
    left_norm = jnp.sum(left_rows * left_rows, axis=-1, keepdims=True)
    right_norm = jnp.sum(right_rows * right_rows, axis=-1, keepdims=True)
    left_coef = 1.0 - cross_term / (2.0 * (left_norm + norm_epsilon))
    right_coef = 1.0 - cross_term / (2.0 * (right_norm + norm_epsilon))
    return left_coef * left_rows + right_coef * right_rows


def adam_update(gradient, weight_rows, first_rows, second_rows):
    first_new = beta_one * first_rows + (1.0 - beta_one) * gradient
    second_new = beta_two * second_rows + (1.0 - beta_two) * gradient * gradient
    first_hat = first_new / (1.0 - beta_one**step_count)
    second_hat = second_new / (1.0 - beta_two**step_count)
    weight_new = weight_rows - rate_value * first_hat / (jnp.sqrt(second_hat) + adam_epsilon)
    return (weight_new, first_new, second_new)


def prepare_kernel(middle, own, spans, place_ref, tokens_ref, keep_ref, other_ref):
    def fill(mine):
        width = 128
        for base in range(0, tokens_ref.shape[1], width):
            block = tokens_ref[:, base : base + width].T
            for group in range(base // own, (base + width) // own):
                node, here = divmod(group, 2)
                top, mid = divmod(node, middle)
                target = keep_ref if here == mine else other_ref
                for first, piece in spans:
                    row = first * middle * 2 + (mid * 2 + top) * piece
                    low = group * own + first - base
                    target[row : row + piece, :] = block[low : low + piece, :]

    for mine in range(2):
        pl.when(place_ref[CORE] == mine)(functools.partial(fill, mine))


def choose_kernel(place_ref, cotangent_ref, swap_ref, send_ref):
    half = send_ref.shape[0]
    send_ref[...] = jnp.where(place_ref[OWNER] == 1, swap_ref[half:, :], cotangent_ref[:half, :])


def share_kernel(place_ref, keep_ref, swap_ref, near_ref, *send_refs):
    owner = place_ref[OWNER] == 1
    near_ref[...] = jnp.where(owner, keep_ref[...], swap_ref[...])
    row = 0
    for send_ref in send_refs:
        rows = slice(row, row + send_ref.shape[0])
        send_ref[...] = jnp.where(owner, swap_ref[rows, :], keep_ref[rows, :])
        row += send_ref.shape[0]


def project_kernel(place_ref, tokens_ref, cotangent_ref, weight_ref, projected_ref, grad_ref):
    tokens = parts(tokens_ref[...])
    cotangent = parts(cotangent_ref[...])
    width = weight_ref.shape[0]
    step = min(256, width)
    for base in range(0, width, step):
        span = slice(base, base + step)
        projected_ref[:, span] = product(tokens, parts(weight_ref[:, span]))
        grad_ref[:, span] = product(cotangent, parts(weight_ref[span, :]), 1)


def near_kernel(scale, place_ref, tokens_ref, cotangent_ref, swap_ref, near_ref):
    right = parts(jnp.where(place_ref[OWNER] == 1, cotangent_ref[...], swap_ref[...]))
    near_ref[...] = product(parts(tokens_ref[...]), right) * scale


def assemble_kernel(place_ref, mine_ref, other_ref, high_ref, low_ref):
    owner = place_ref[OWNER] == 1
    half = mine_ref.shape[0]
    for at in range(2):
        rows = slice(at * half, (at + 1) * half)
        chosen = jnp.where(owner == (at == 0), mine_ref[...], other_ref[...])
        high_ref[rows, :], low_ref[rows, :] = parts(chosen)


def halves(place_ref, bit, start, half):
    mine = place_ref[BITS + bit]
    return [(start, part, half) for part in (mine, 1 - mine)]


def taken(ref, rows):
    start, part, half = rows
    if half % 8 == 0:
        return ref[pl.ds(pl.multiple_of(start + part * half, half), half), :]
    return jnp.where(part == 1, ref[start + half : start + 2 * half, :], ref[start : start + half, :])


def first_kernel(scale, bit, near_start, far_start, place_ref, near_ref, far_ref, high_ref, low_ref, keep_ref, send_ref):
    right = (high_ref[...], low_ref[...])
    half = keep_ref.shape[0]
    near_rows = halves(place_ref, bit, near_start, half)
    far_rows = halves(place_ref, bit, far_start, half)
    for target, at in ((send_ref, 1), (keep_ref, 0)):
        far = product(parts(taken(far_ref, far_rows[at])), right) * scale
        target[...] = combine(taken(near_ref, near_rows[at]), far)


def middle_kernel(bit, segment, place_ref, *refs):
    *pairs, keep_ref, send_ref = refs
    half = segment // 2
    out = 0
    for kept_ref, received_ref in zip(pairs[::2], pairs[1::2]):
        for start in range(0, kept_ref.shape[0], segment):
            for target, rows in zip((keep_ref, send_ref), halves(place_ref, bit, start, half)):
                target[out : out + half, :] = combine(taken(kept_ref, rows), taken(received_ref, rows))
            out += half


def last_kernel(
    spans, place_ref, kept_ref, received_ref, weight_ref, first_ref, second_ref,
    weight_out, first_out, second_out,
):
    first, rows = spans[0][0], kept_ref.shape[0]
    span = slice(first, first + rows)
    weight_out[...], first_out[...], second_out[...] = adam_update(
        combine(kept_ref[...], received_ref[...]), weight_ref[span, :], first_ref[span, :], second_ref[span, :]
    )


def pair_kernel(place_ref, *refs):
    *row_refs, out_ref = refs
    half = out_ref.shape[0] // 2
    count = len(row_refs) // 2
    top = place_ref[TOP]
    for side, group in ((top, row_refs[:count]), (1 - top, row_refs[count:])):
        start = 0
        for row_ref in group:
            rows = row_ref.shape[0]
            out_ref[pl.ds(pl.multiple_of(side * half + start, rows), rows), :] = row_ref[...]
            start += rows


def finish_kernel(middle, own, streams, place_ref, tokens_ref, *refs):
    *block_refs, weight_ref, projected_ref = refs
    mid, core = place_ref[MIDDLE], place_ref[CORE]
    for at, block_ref in enumerate(block_refs):
        stream, at = divmod(at, 2 * middle)
        far_mid, far_core = divmod(at, 2)
        device = (mid ^ far_mid) * 2 + (core ^ far_core)
        first, rows = streams[stream][0][0], block_ref.shape[0] // 2
        for top in range(2):
            row = (device + top * middle * 2) * own + first
            weight_ref[pl.ds(pl.multiple_of(row, 8), rows), :] = block_ref[top * rows : (top + 1) * rows, :]
    depth = min(256, tokens_ref.shape[1])
    total = jnp.zeros(projected_ref.shape, jnp.float32)
    for base in range(0, tokens_ref.shape[1], depth):
        span = slice(base, base + depth)
        total = total + product(parts(tokens_ref[:, span]), parts(weight_ref[span, :]))
    projected_ref[...] = total


def relative_blocks(rows, bits, load, direct):
    blocks = {0: rows}
    masks = [sum(1 << bits[at] for at in range(len(bits)) if pick >> at & 1) for pick in range(1, 1 << len(bits))]
    for mask in sorted(masks, key=lambda mask: mask.bit_count()):
        inside = [bit for bit in bits if mask >> bit & 1]
        if direct and len(inside) > 2:
            blocks[mask] = swapped(rows, mask)
            continue
        if mask.bit_count() == 2 and len(bits) == 3:
            at = bits.index(inside[0])
            last = inside[1] if bits[(at + 1) % 3] == inside[1] else inside[0]
        else:
            last = min(inside, key=lambda bit: load[bit])
        load[last] += 1
        blocks[mask] = swapped(blocks[mask ^ 1 << last], 1 << last)
    return blocks


def on_device(tokens, cotangent, weight, first_moment, second_moment):
    token_count, width = tokens.shape
    devices = lax.axis_size("dp")
    levels = devices.bit_length() - 1
    index = lax.axis_index("dp")
    own = width // devices
    middle = devices // 4
    units = 4 if own % 32 == 0 else 1
    piece = own // units
    spans = [(at * piece, piece) for at in range(units)]
    messages = MESSAGES if units == 4 else [[0]]
    groups = GROUPS if units == 4 else [[0]]
    streams = [[spans[unit] for unit in group] for group in groups]
    top_mask = devices >> 1
    core, top = index & 1, index >> levels - 1
    scale = 1.0 / token_count
    place = jnp.stack(
        [(core == top).astype(jnp.int32), top, index >> 1 & middle - 1, core]
        + [index >> bit & 1 for bit in range(levels)]
    )
    half_rows = width // 2

    cotangent_swap = swapped(cotangent, 1)
    tokens_keep, tokens_other = kernel_call(
        functools.partial(prepare_kernel, middle, own, spans), "prepare",
        [f32(half_rows, token_count)] * 2, 4, place, tokens,
    )
    tokens_swap = swapped(tokens_other, 1)
    (send_cotangent,) = kernel_call(
        choose_kernel, "choose", [f32(token_count // 2, width)], 4, place, cotangent, cotangent_swap
    )
    far_mine = swapped(send_cotangent, top_mask)
    unit_rows = half_rows // units
    near_tokens, *send_tokens = kernel_call(
        share_kernel, "share",
        [f32(half_rows, token_count)] + [f32(unit_rows * len(message), token_count) for message in messages],
        4, place, tokens_keep, tokens_swap,
    )
    far_tokens = [swapped(block, top_mask) for block in send_tokens]
    (near,) = kernel_call(
        functools.partial(near_kernel, scale), "near", [f32(half_rows, width)], 12,
        place, near_tokens, cotangent, cotangent_swap,
    )
    projected, input_grad = kernel_call(
        project_kernel, "project", [f32(token_count, width)] * 2, 20, place, tokens, cotangent, weight,
        after=(near_tokens,),
    )
    weight_rows = lax.dynamic_slice_in_dim(weight, index * own, own, 0)
    near, projected, input_grad, weight_rows, far_mine, far_tokens[0] = lax.optimization_barrier(
        (near, projected, input_grad, weight_rows, far_mine, far_tokens[0])
    )
    far_main, far_rest = kernel_call(
        assemble_kernel, "assemble", [bf16(token_count, width)] * 2, 6, place, far_mine, swapped(far_mine, 1)
    )

    bits = list(range(levels - 2, 0, -1)) + [levels - 1]
    firsts = {}
    for message, far in zip(messages, far_tokens):
        for at, unit in enumerate(message):
            firsts[unit] = kernel_call(
                functools.partial(first_kernel, scale, bits[0], unit * unit_rows, at * unit_rows), "first",
                [f32(unit_rows // 2, width)] * 2, 8, place, near, far, far_main, far_rest,
            )
    state = [[firsts[unit] for unit in group] for group in groups]
    outs, after = {}, tuple(firsts[unit][0] for unit in range(units))
    order = [(k, level) for level in range(1, levels) for k in range(len(groups))]
    if len(groups) == 2 and levels == 5:
        order = ORDER
    arrived = [[swapped(send, 1 << bits[0]) for _, send in pairs] for pairs in state]
    after += tuple(block for blocks in arrived[1:] for block in blocks[:AHEAD])
    for k, level in order:
        count = len(groups[k])
        segment = unit_rows >> level
        operands = [place]
        for at, (keep, send) in enumerate(state[k]):
            operands += [keep, arrived[k][at] if level == 1 else swapped(send, 1 << bits[level - 1])]
        if level == levels - 1:
            outs[k] = kernel_call(
                functools.partial(last_kernel, streams[k]), "last", [f32(piece * count, width)] * 3, 4, *operands,
                weight_rows, first_moment, second_moment, after=after,
            )
            after = (outs[k][0],)
            continue
        made = kernel_call(
            functools.partial(middle_kernel, bits[level], segment), "middle",
            [f32(segment // 2 * count, width)] * 2, 8, *operands, after=after,
        )
        state[k] = [made]
        after = (made[0],)
    outs = [outs[k] for k in range(len(groups))]
    new_rows, new_first, new_second = zip(*outs)
    new_first = jnp.concatenate(new_first, axis=0)
    new_second = jnp.concatenate(new_second, axis=0)

    if devices > 64:
        mine = jnp.concatenate(new_rows, axis=0)
        new_weight = lax.all_gather(mine, "dp", axis=0, tiled=True)
        next_projected = jnp.dot(
            tokens, new_weight, precision=lax.Precision.HIGH, preferred_element_type=jnp.float32
        )
        return (projected, input_grad, new_weight, new_first, new_second, next_projected)

    order = list(range(levels - 2, 0, -1))
    load = dict.fromkeys(order, 0)
    blocks = []
    if JOIN:
        streams, sets = [sum(streams, [])], [list(new_rows)]
    else:
        sets = [[rows] for rows in new_rows]
    for at, rows in enumerate(sets):
        (both,) = kernel_call(
            pair_kernel, "pair", [f32(2 * sum(block.shape[0] for block in rows), width)], 4, place,
            *rows, *(swapped(block, top_mask) for block in rows),
        )
        if FRESH:
            load = dict.fromkeys(order, 0)
        found = relative_blocks(both, order, load, at >= DIRECT)
        for mid in range(middle):
            blocks += [found[mid << 1], swapped(found[mid << 1], 1)]
    new_weight, next_projected = kernel_call(
        functools.partial(finish_kernel, middle, own, streams), "finish",
        [f32(width, width), f32(token_count, width)], 28, place, tokens, *blocks,
    )
    return (projected, input_grad, new_weight, new_first, new_second, next_projected)


def solution(mesh):
    split, whole = P("dp", None), P()
    return jax.shard_map(
        on_device,
        mesh=mesh,
        in_specs=(split, split, whole, split, split),
        out_specs=(split, split, whole, split, split, split),
        check_vma=False,
    )
```
